512 devices in a mesh: src: 128 (over z, y, core), tgt: 4 (over x).
Axes of the slice: x: 4, y: 4, z: 16, core: 2. Of those that a mesh axis runs over, the one named last changes fastest.
Arguments:
- source_mean: float32 [16, 32768], P(None, 'src'), may hold values from -1 to 1, as said below
- target_points: float32 [16, 16384], P(None, 'tgt'), may hold values from -1 to 1
- precision: float32 [16], replicated, may hold values from 0.25 to 2, as said below
- target_values: float32 [16384, 128], P('tgt'), may hold values from 0.5 to 3
- cash: float32 [32768, 128], P('src'), may hold values from -3 to 3
- salvage: float32 [32768, 128], P('src'), may hold values from 0.5 to 3
- switch_cost: float32 [128], replicated, may hold values from 0.05 to 0.5
- cotangent: float32 [32768, 128], P('src'), may hold values from -0.5 to 1.5
- decision: int32 [32768, 128], P('src'), may hold values from 0 to 2
Outputs:
- source_value: float32 [32768, 128], P('src')
- target_adjoint: float32 [4, 4096, 128], P('tgt', 'src')
The draws below stay inside these ranges and needn't reach their ends.
Inputs may be any that keep to these rules, and one draw needn't show every extreme that they name: `source_mean`: the first factor of source i lies between -1 + 2 i / 32768 and -1 + 2 (i + 1) / 32768. The first factor's precision is 1.5 or more.
All inputs are finite; a program needn't handle non-finite values.
Results may differ from the reference program's by a relative error of at most 0.00024.
Values sent between devices are 32-bit elements; how exact they have to be, the bound alone decides.
A program may use at most 64 MiB of HBM per device.

```python
import math
import jax
import jax.numpy as jnp
from jax import lax

F = 16
M = 128
SRC_DEV = 256
TGT_DEV = 4096
NS = 32768
NT = 16384
N_SRC = 128


def draw_source_mean(key, part):
    first_key, second_key = jax.random.split(key)
    jitter = jax.random.uniform(first_key, (NS,), jnp.float32)
    leading = -1.0 + 2.0 * (jnp.arange(NS, dtype=jnp.float32) + jitter) / NS
    leading = jnp.clip(leading, -1.0, 1.0)
    others = jax.random.uniform(second_key, (F - 1, NS), jnp.float32, minval=-1.0, maxval=1.0)
    return jnp.concatenate([leading[None, :], others], axis=0)


def draw_precision(key, part):
    first_key, second_key = jax.random.split(key)
    leading = jax.random.uniform(first_key, (1,), jnp.float32, minval=1.5, maxval=2.0)
    others = jnp.exp(jax.random.uniform(second_key, (F - 1,), jnp.float32, minval=math.log(0.25), maxval=math.log(2.0)))
    return jnp.concatenate([leading, others], axis=0)


def plant(drawn, rng, smallest, top_value):
    dims = drawn.shape
    place = [jax.random.randint(jax.random.fold_in(rng, axis), (), 0, dims[axis]) for axis in range(len(dims))]
    drawn = drawn.at[tuple(place)].set(smallest)
    longest = dims.index(max(dims))
    place[longest] = (place[longest] + 1) % dims[longest]
    return drawn.at[tuple(place)].set(top_value)


def shard_levels(stream_key, shape, cuts, smallest, top_value):
    level, own = 1.0, jax.random.fold_in(stream_key, 6)
    for dim, parts in cuts:
        steps = jnp.exp(jax.random.uniform(jax.random.fold_in(own, dim), (parts,), jnp.float32, smallest / len(cuts), top_value / len(cuts)))
        level = level * jnp.repeat(steps, shape[dim] // parts).reshape([-1 if axis == dim else 1 for axis in range(len(shape))])
    return level


def noise(key, shape, deviation, limit, cuts=(), kind=jnp.bfloat16):
    gain = shard_levels(key, shape, cuts, -0.22, 0.18) if cuts else 1.0
    drawn = jax.random.normal(key, shape, jnp.float32) * deviation * gain
    return jnp.minimum(jnp.maximum(drawn, -limit), limit).astype(kind)


def setup_inputs(seed: int = 0) -> dict:
    keys = jax.random.split(jax.random.key(seed), 10)
    return {
        "source_mean": draw_source_mean(jax.random.fold_in(keys[9], 71), 0),
        "target_points": jnp.clip(jax.random.uniform(keys[1], (F, NT), jnp.float32, -1.0, 1.0) * shard_levels(keys[1], (F, NT), ((1, 4),), -0.4, 0.0), -1.0, 1.0),
        "precision": draw_precision(jax.random.fold_in(keys[9], 71), 0),
        "target_values": jnp.clip(0.5 + 2.5 * jax.random.uniform(keys[3], (NT, M), jnp.float32) ** shard_levels(keys[3], (NT, M), ((0, 4),), -0.2, 0.2), 0.5, 3.0),
        "cash": noise(keys[4], (NS, M), 0.5, 3.0, ((0, 128),), jnp.float32),
        "salvage": jnp.clip(0.5 + 2.5 * jax.random.uniform(keys[5], (NS, M), jnp.float32) ** shard_levels(keys[5], (NS, M), ((0, 128),), -0.2, 0.2), 0.5, 3.0),
        "switch_cost": jnp.clip(jnp.exp(jax.random.uniform(keys[6], (M,), jnp.float32, math.log(0.05), math.log(0.5))), 0.05, 0.5),
        "cotangent": jnp.clip(-0.5 + 2.0 * jax.random.uniform(keys[7], (NS, M), jnp.float32) ** shard_levels(keys[7], (NS, M), ((0, 128),), -0.2, 0.2), -0.5, 1.5),
        "decision": plant(jax.random.randint(keys[8], (NS, M), 0, 3), jax.random.fold_in(keys[8], 1), 0, 2).astype(jnp.int32),
    }


def choose_value(continuation, cash_part, salvage_part, cost_part):
    hold_value = continuation + cash_part
    paired = hold_value.reshape(hold_value.shape[0], -1, 2)[:, :, ::-1].reshape(hold_value.shape)
    switched = paired - cost_part[None, :]
    return jnp.maximum(jnp.maximum(hold_value, switched), salvage_part)


def adjoint_input(cotangent, decision):
    held = jnp.where(decision == 0, cotangent, 0.0)
    moved = jnp.where(decision == 1, cotangent, 0.0)
    swapped = moved.reshape(moved.shape[0], -1, 2)[:, :, ::-1].reshape(moved.shape)
    return held + swapped


def block_density(scaled_part, offset_part, target_points):
    cross = lax.dot_general(scaled_part, target_points, (((0,), (0,)), ((), ())), precision=lax.Precision.HIGHEST, preferred_element_type=jnp.float32)
    return jnp.exp(cross + offset_part[:, None])


def reference(source_mean, target_points, precision, target_values, cash, salvage, switch_cost, cotangent, decision):
    scaled = source_mean * precision[:, None]
    offset = -0.5 * jnp.sum(scaled * source_mean, axis=0)
    scaled_blocks = scaled.reshape(F, N_SRC, SRC_DEV).transpose(1, 0, 2)
    offset_blocks = offset.reshape(N_SRC, SRC_DEV)
    adjoint_in = adjoint_input(cotangent, decision)
    adjoint_blocks = adjoint_in.reshape(N_SRC, SRC_DEV, M)

    def add_columns(running, pieces):
        dens_block = block_density(pieces[0], pieces[1], target_points)
        return running + jnp.sum(dens_block, axis=0), None

    column_sum, _ = lax.scan(add_columns, jnp.zeros((NT,), jnp.float32), (scaled_blocks, offset_blocks))
    factor = (NS / NT) / column_sum
    scaled_values = target_values * factor[:, None]

    def both_products(running, pieces):
        dens_block = block_density(pieces[0], pieces[1], target_points)
        cont_block = jnp.dot(dens_block, scaled_values, precision=lax.Precision.HIGHEST, preferred_element_type=jnp.float32)
        back_part = lax.dot_general(dens_block, pieces[2], (((0,), (0,)), ((), ())), precision=lax.Precision.HIGHEST, preferred_element_type=jnp.float32)
        return running + back_part, cont_block

    raw_sum, cont_blocks = lax.scan(both_products, jnp.zeros((NT, M), jnp.float32), (scaled_blocks, offset_blocks, adjoint_blocks))
    continuation = cont_blocks.reshape(NS, M)
    source_value = choose_value(continuation, cash, salvage, switch_cost)
    target_adjoint = (raw_sum * factor[:, None]).reshape(NT // TGT_DEV, TGT_DEV, M)
    return source_value, target_adjoint
```

```python
import functools
import math

import jax
import jax.numpy as jnp
from jax import lax
from jax.experimental import pallas as pl
from jax.experimental.pallas import tpu as pltpu
from jax.sharding import PartitionSpec as P

F32, BF16 = jnp.float32, jnp.bfloat16
MESH = pl.DeviceIdType.MESH
LOG2E = math.log2(math.e)


def split2(v):
    hi = v.astype(BF16)
    return hi, (v - hi.astype(F32)).astype(BF16)


def split3(v):
    hi = v.astype(BF16)
    rest = v - hi.astype(F32)
    mid = rest.astype(BF16)
    return hi, mid, (rest - mid.astype(F32)).astype(BF16)


def beside(v):
    hi, lo = split2(v)
    return jnp.concatenate([hi, lo], axis=1)


def source_stack(mean, prec_col):
    scaled = mean * prec_col
    offset = jnp.sum(scaled * mean, axis=0, keepdims=True) * (-0.5 * LOG2E)
    a, b, c = split3(scaled * LOG2E)
    p, q, r = split3(offset)
    row = lax.broadcasted_iota(jnp.int32, mean.shape, 0)
    tail = jnp.where(
        row == 0, p.astype(F32), jnp.where(row == 1, q.astype(F32), jnp.where(row == 2, r.astype(F32), 0.0))
    ).astype(BF16)
    return jnp.concatenate([a, a, b, a, b, c, tail], axis=0)


def target_stack(points):
    a, b, c = split3(points)
    row = lax.broadcasted_iota(jnp.int32, points.shape, 0)
    tail = jnp.where(row < 3, 1.0, 0.0).astype(BF16)
    return jnp.concatenate([a, b, a, c, b, a, tail], axis=0)


def pair_swap(v):
    lane = lax.broadcasted_iota(jnp.int32, v.shape, 1)
    width = v.shape[1]
    return jnp.where(lane % 2 == 0, pltpu.roll(v, width - 1, 1), pltpu.roll(v, 1, 1))


def tdot(a, b):
    return lax.dot_general(a, b, (((0,), (0,)), ((), ())), preferred_element_type=F32)


def dot(a, b):
    return jnp.dot(a, b, preferred_element_type=F32)


def kernel(
    dims,
    scale,
    mean_h, points_h, prec_s, values_h, cash_h, salvage_h, cost_v, cot_h, dec_h,
    value_out, adjoint_out,
    mean_v, adj, cot_v, dec_v, points_v, values_v, cash_v, salvage_v,
    dens, sstack, tstack, t2, vstack, acc,
    colpart, rs_buf, zc_src, zc_buf, col_all,
    sib_src, sib_buf, zb_src, zb_buf,
    xr_src, xr_buf, value_v,
    ld_sem, g_send, g_recv, rs_send, rs_recv, zc_send, zc_recv, ag_send, ag_recv,
    sib_send, sib_recv, zb_send, zb_recv, xr_send, xr_recv, xa_send, xa_recv,
):
    Z, Y, C, X = dims
    W = Y * C
    S, M = cot_v.shape
    T = points_v.shape[1]
    TW = T // W
    R = T // (Z * W)
    S4 = S // X
    s = lax.axis_index("src")
    x = lax.axis_index("tgt")
    z, w = s // W, s % W
    y, c = w // C, w % C

    def at_z(i):
        return (((z + i) % Z) * W + w, x)

    def at_w(i):
        return (z * W + (w + i) % W, x)

    def at_y(i):
        return (z * W + ((y + i) % Y) * C + c, x)

    def at_x(i):
        return (s, (x + i) % X)

    sibling = (z * W + y * C + (1 - c), x)

    def remote(src, dst, send, recv, dev):
        cp = pltpu.make_async_remote_copy(
            src_ref=src, dst_ref=dst, send_sem=send, recv_sem=recv, device_id=dev, device_id_type=MESH
        )
        cp.start()
        return cp

    def near_far(n):
        return sorted(range(1, n), key=lambda i: -min(i, n - i))

    loads = {}
    for k, (name, src, dst) in enumerate([
        ("cot", cot_h, cot_v), ("dec", dec_h, dec_v), ("mean", mean_h, mean_v.at[0]), ("points", points_h, points_v),
        ("values", values_h, values_v), ("cash", cash_h, cash_v), ("salvage", salvage_h, salvage_v),
    ]):
        loads[name] = pltpu.make_async_copy(src, dst, ld_sem.at[k])
        loads[name].start()

    barrier = pltpu.get_barrier_semaphore()
    peers = [at_w(i) for i in range(1, W)] + [at_z(i) for i in range(1, Z)] + [at_x(i) for i in range(1, X)]
    for dev in peers:
        pl.semaphore_signal(barrier, inc=1, device_id=dev, device_id_type=MESH)

    loads["cot"].wait()
    loads["dec"].wait()
    cot = cot_v[...]
    dec = dec_v[...]
    adj[0] = jnp.where(dec == 0, cot, 0.0) + pair_swap(jnp.where(dec == 1, cot, 0.0))
    loads["mean"].wait()
    frow = lax.broadcasted_iota(jnp.int32, (mean_v.shape[1], 1), 0)
    prec_col = jnp.zeros((mean_v.shape[1], 1), F32)
    for f in range(mean_v.shape[1]):
        prec_col = jnp.where(frow == f, prec_s[f], prec_col)

    pl.semaphore_wait(barrier, len(peers))

    sends = []
    gathers = {}
    for i in sorted(range(1, Y), key=lambda i: min(i, Y - i)):
        gathers[i] = [
            remote(mean_v.at[0], mean_v.at[i], g_send.at[i, 0], g_recv.at[i, 0], at_y(i)),
            remote(adj.at[0], adj.at[i], g_send.at[i, 1], g_recv.at[i, 1], at_y(i)),
        ]
        sends += gathers[i]

    sstack[0] = source_stack(mean_v[0], prec_col)
    loads["points"].wait()

    def first_density(j, carry):
        cols = pl.ds(pl.multiple_of(j * TW, TW), TW)
        tstack_j = target_stack(points_v[:, cols])
        d = jnp.exp2(tdot(sstack[0], tstack_j))
        dens[:, cols] = d
        colpart[j] = jnp.sum(d, axis=0, keepdims=True)
        return carry

    lax.fori_loop(0, W, first_density, 0)

    rs = []
    for i in range(1, W):
        rs.append(remote(colpart.at[(w + i) % W], rs_buf.at[i], rs_send.at[i], rs_recv.at[i], at_w(i)))
    sends += rs

    width = min(128, Z * R)
    lane = lax.broadcasted_iota(jnp.int32, (mean_v.shape[1], width), 1)
    per = width // R
    for half in range(2):
        core = (c + 1 + half) % C
        blocks = []
        for g in range(Z // per):
            block = jnp.zeros((mean_v.shape[1], width), F32)
            for k in range(per):
                off = (g * per + k) * (W * R) + (y * C + core) * R
                base = pl.multiple_of(off // width * width, width)
                turn = (k * R + width - off % width) % width
                piece = pltpu.roll(points_v[:, pl.ds(base, width)], turn, 1)
                block = jnp.where((lane >= k * R) & (lane < (k + 1) * R), piece, block)
            blocks.append(block)
        t2[half] = target_stack(jnp.concatenate(blocks, axis=1))

    for cp in rs:
        cp.wait_recv()
    total = colpart[w]
    for i in range(1, W):
        total = total + rs_buf[i]
    zc_src[...] = total
    zc_buf[0] = total
    zc = []
    for i in near_far(Z):
        zc.append(remote(zc_src, zc_buf.at[i], zc_send.at[i], zc_recv.at[i], at_z(i)))
    sends += zc

    def back_block(i, half, first):
        d = jnp.exp2(tdot(t2[half], sstack[i]))
        hi, lo = split2(d)
        a = beside(adj[i])
        term = dot(hi, a) + dot(lo, a)
        acc[half] = term if first else acc[half] + term

    back_block(0, 0, True)
    back_block(0, 1, True)

    loads["values"].wait()

    def stack_values(j, carry):
        rows = pl.ds(pl.multiple_of(j * TW, TW), TW)
        vstack[rows, :] = beside(values_v[rows, :])
        return carry

    lax.fori_loop(0, W, stack_values, 0)

    for cp in zc:
        cp.wait_recv()
    total = zc_buf[0]
    for i in range(1, Z):
        total = total + zc_buf[i]
    col_all[w] = total
    ag = []
    for i in range(1, W):
        ag.append(remote(col_all.at[w], col_all.at[w], ag_send.at[i], ag_recv.at[i], at_w(i)))
    sends += ag

    order = sorted(range(1, Y), key=lambda i: min(i, Y - i))
    for n, i in enumerate(order):
        for cp in gathers[i]:
            cp.wait_recv()
        sstack[i] = source_stack(mean_v[i], prec_col)
        back_block(i, 0, False)
        if n == len(order) - 1:
            sib_src[...] = acc[0, :, :M] + acc[0, :, M:]
            sib = remote(sib_src, sib_buf, sib_send, sib_recv, sibling)
            sends.append(sib)
        back_block(i, 1, False)

    own = acc[1, :, :M] + acc[1, :, M:]
    sib.wait_recv()
    own = own + sib_buf[...]
    zb_src[...] = own.reshape(Z, R, M)
    zb = []
    for i in near_far(Z):
        zb.append(remote(zb_src.at[(z + i) % Z], zb_buf.at[i], zb_send.at[i], zb_recv.at[i], at_z(i)))
    sends += zb

    for cp in ag:
        cp.wait_recv()

    def forward(j, total):
        cols = pl.ds(pl.multiple_of(j * TW, TW), TW)
        hi, lo = split2(dens[:, cols] * (scale / col_all[j]))
        v = vstack[cols, :]
        return total + dot(hi, v) + dot(lo, v)

    both = lax.fori_loop(0, W, forward, jnp.zeros((S, 2 * M), F32))
    xr_src[...] = (both[:, :M] + both[:, M:]).reshape(X, S4, M)
    xr = []
    for i in near_far(X):
        xr.append(remote(xr_src.at[(x + i) % X], xr_buf.at[i], xr_send.at[i], xr_recv.at[i], at_x(i)))
    sends += xr
    loads["cash"].wait()
    loads["salvage"].wait()
    for cp in xr:
        cp.wait_recv()
    rows = pl.ds(pl.multiple_of(x * S4, S4), S4)
    hold = xr_src[x]
    for i in range(1, X):
        hold = hold + xr_buf[i]
    hold = hold + cash_v[rows, :]
    value_v[x] = jnp.maximum(jnp.maximum(hold, pair_swap(hold) - cost_v[...]), salvage_v[rows, :])
    xa = []
    for i in near_far(X):
        xa.append(remote(value_v.at[x], value_v.at[x], xa_send.at[i], xa_recv.at[i], at_x(i)))
    sends += xa

    own_off = s * R
    jw = own_off // TW
    inner = own_off % TW
    win = min(128, TW)
    base = pl.multiple_of(inner // win * win, win)
    line = col_all[jw, :, pl.ds(base, win)]
    r_iota = lax.broadcasted_iota(jnp.int32, (R, win), 0)
    l_iota = lax.broadcasted_iota(jnp.int32, (R, win), 1)
    own_sum = jnp.sum(jnp.where(l_iota == r_iota + inner % win, line, 0.0), axis=1, keepdims=True)
    own_factor = scale / own_sum

    for cp in zb:
        cp.wait_recv()
    raw = zb_src[z]
    for i in range(1, Z):
        raw = raw + zb_buf[i]
    adjoint_out[0] = raw * own_factor

    for cp in xa:
        cp.wait_recv()
    value_out[...] = value_v[...].reshape(S, M)
    for cp in sends:
        cp.wait_send()


def on_device(dims, mean, points, precision, values, cash, salvage, cost, cot, dec):
    Z, Y, C, X = dims
    W = Y * C
    F, S = mean.shape
    T = points.shape[1]
    M = cot.shape[1]
    R, TW, K = T // (Z * W), T // W, 7 * F
    scale = float(S * Z * W) / float(T * X)
    hbm = pl.BlockSpec(memory_space=pltpu.HBM)
    vmem = pl.BlockSpec(memory_space=pltpu.VMEM)
    dma = pltpu.SemaphoreType.DMA
    scratch = [
        pltpu.VMEM((Y, F, S), F32), pltpu.VMEM((Y, S, M), F32), pltpu.VMEM((S, M), F32), pltpu.VMEM((S, M), jnp.int32),
        pltpu.VMEM((F, T), F32), pltpu.VMEM((T, M), F32), pltpu.VMEM((S, M), F32), pltpu.VMEM((S, M), F32),
        pltpu.VMEM((S, T), F32), pltpu.VMEM((Y, K, S), BF16), pltpu.VMEM((16, 128), BF16), pltpu.VMEM((2, K, Z * R), BF16),
        pltpu.VMEM((T, 2 * M), BF16), pltpu.VMEM((2, Z * R, 2 * M), F32),
        pltpu.VMEM((W, 1, TW), F32), pltpu.VMEM((W, 1, TW), F32), pltpu.VMEM((1, TW), F32), pltpu.VMEM((Z, 1, TW), F32),
        pltpu.VMEM((W, 1, TW), F32),
        pltpu.VMEM((Z * R, M), F32), pltpu.VMEM((Z * R, M), F32), pltpu.VMEM((Z, R, M), F32), pltpu.VMEM((Z, R, M), F32),
        pltpu.VMEM((X, S // X, M), F32), pltpu.VMEM((X, S // X, M), F32), pltpu.VMEM((X, S // X, M), F32),
        dma((7,)), dma((Y, 2)), dma((Y, 2)), dma((W,)), dma((W,)), dma((Z,)), dma((Z,)), dma((W,)), dma((W,)),
        dma, dma, dma((Z,)), dma((Z,)), dma((X,)), dma((X,)), dma((X,)), dma((X,)),
    ]
    return pl.pallas_call(
        functools.partial(kernel, dims, scale),
        out_shape=(jax.ShapeDtypeStruct((S, M), F32), jax.ShapeDtypeStruct((1, R, M), F32)),
        in_specs=[hbm, hbm, pl.BlockSpec(memory_space=pltpu.SMEM), hbm, hbm, hbm, vmem, hbm, hbm],
        out_specs=(vmem, vmem),
        scratch_shapes=scratch,
        compiler_params=pltpu.CompilerParams(
            collective_id=0, has_side_effects=True, vmem_limit_bytes=60 * 1024 * 1024
        ),
        name="mesh_step",
    )(mean, points, precision, values, cash, salvage, cost.reshape(1, M), cot, dec)


def build(mesh, dims):
    placed = (
        P(None, "src"), P(None, "tgt"), P(), P("tgt", None), P("src", None), P("src", None), P(), P("src", None),
        P("src", None),
    )
    return jax.shard_map(
        functools.partial(on_device, dims),
        mesh=mesh,
        in_specs=placed,
        out_specs=(P("src", None), P("tgt", "src", None)),
        check_vma=False,
    )


def solution(mesh):
    src, tgt = mesh.shape["src"], mesh.shape["tgt"]
    return build(mesh, (src // 8, 4, 2, tgt))
```

```python
import functools
import math

import jax
import jax.numpy as jnp
from jax import lax
from jax.experimental import pallas as pl
from jax.experimental.pallas import tpu as pltpu
from jax.sharding import PartitionSpec as P

F32, BF16 = jnp.float32, jnp.bfloat16
MESH = pl.DeviceIdType.MESH
LOG2E = math.log2(math.e)


def split2(v):
    hi = v.astype(BF16)
    return hi, (v - hi.astype(F32)).astype(BF16)


def split3(v):
    hi = v.astype(BF16)
    rest = v - hi.astype(F32)
    mid = rest.astype(BF16)
    return hi, mid, (rest - mid.astype(F32)).astype(BF16)


def beside(v):
    hi, lo = split2(v)
    return jnp.concatenate([hi, lo], axis=1)


def source_stack(mean, prec_col):
    scaled = mean * prec_col
    offset = jnp.sum(scaled * mean, axis=0, keepdims=True) * (-0.5 * LOG2E)
    a, b, c = split3(scaled * LOG2E)
    p, q, r = split3(offset)
    row = lax.broadcasted_iota(jnp.int32, mean.shape, 0)
    tail = jnp.where(
        row == 0, p.astype(F32), jnp.where(row == 1, q.astype(F32), jnp.where(row == 2, r.astype(F32), 0.0))
    ).astype(BF16)
    return jnp.concatenate([a, a, b, a, b, c, tail], axis=0)


def target_stack(points):
    a, b, c = split3(points)
    row = lax.broadcasted_iota(jnp.int32, points.shape, 0)
    tail = jnp.where(row < 3, 1.0, 0.0).astype(BF16)
    return jnp.concatenate([a, b, a, c, b, a, tail], axis=0)


def pair_swap(v):
    lane = lax.broadcasted_iota(jnp.int32, v.shape, 1)
    width = v.shape[1]
    return jnp.where(lane % 2 == 0, pltpu.roll(v, width - 1, 1), pltpu.roll(v, 1, 1))


def tdot(a, b):
    return lax.dot_general(a, b, (((0,), (0,)), ((), ())), preferred_element_type=F32)


def dot(a, b):
    return jnp.dot(a, b, preferred_element_type=F32)


def kernel(
    dims,
    scale,
    mean_h, points_h, prec_h, values_h, cash_h, salvage_h, cost_h, cot_h, dec_h,
    value_out, adjoint_out,
    mean_v, adj, cot_v, dec_v, points_v, values_v, cash_v, salvage_v, prec_s, cost_v,
    dens, sstack, t2, vstack, acc,
    colpart, rs_buf, zc_src, zc_buf, col_all,
    sib_src, sib_buf, own_v, z_src, z1_buf, z2_src, z2_buf,
    xr_src, xr_buf, value_v,
    ld_sem, g_send, g_recv, rs_send, rs_recv, zc_send, zc_recv, ag_send, ag_recv,
    sib_send, sib_recv, z1_send, z1_recv, z2_send, z2_recv, xr_send, xr_recv, xa_send, xa_recv, far_sem,
):
    Z, Y, C, X = dims
    W = Y * C
    S, M = cot_v.shape
    F, T = points_v.shape
    TW = T // W
    R = T // (Z * W)
    S4 = S // X
    H = Z // 2
    NEAR = 4
    s = lax.axis_index("src")
    x = lax.axis_index("tgt")
    z, w = s // W, s % W
    y, c = w // C, w % C

    def at_z(i):
        return (((z + i + Z) % Z) * W + w, x)

    def place(i, k):
        return ((y + i) % Y) * C + (c + k) % C

    def at_w(i, k):
        return (z * W + place(i, k), x)

    def at_x(i):
        return (s, (x + i) % X)

    def remote(src, dst, send, recv, dev):
        cp = pltpu.make_async_remote_copy(
            src_ref=src, dst_ref=dst, send_sem=send, recv_sem=recv, device_id=dev, device_id_type=MESH
        )
        cp.start()
        return cp

    def far_first(n):
        return sorted(range(1, n), key=lambda i: -min(i, n - i))

    near_y = sorted(range(1, Y), key=lambda i: min(i, Y - i))
    plane = [(i, k) for i in reversed(near_y) for k in range(C)] + [(0, k) for k in range(1, C)]

    loads = {}

    def load(k, name, src, dst):
        loads[name] = pltpu.make_async_copy(src, dst, ld_sem.at[k])
        loads[name].start()

    load(0, "prec", prec_h, prec_s)
    load(1, "mean", mean_h, mean_v.at[0])
    load(2, "points", points_h, points_v)
    load(3, "cot", cot_h, cot_v)
    load(4, "dec", dec_h, dec_v)

    barrier = pltpu.get_barrier_semaphore()
    near_z = [i for i in far_first(Z) if min(i, Z - i) <= NEAR]
    peers = [at_z(i) for i in near_z] + [at_w(i, k) for i, k in plane] + [at_x(i) for i in far_first(X)]
    for dev in peers:
        pl.semaphore_signal(barrier, inc=1, device_id=dev, device_id_type=MESH)

    loads["prec"].wait()
    loads["mean"].wait()
    frow = lax.broadcasted_iota(jnp.int32, (F, 1), 0)
    prec_col = jnp.zeros((F, 1), F32)
    for f in range(F):
        prec_col = jnp.where(frow == f, prec_s[f], prec_col)
    sstack[0] = source_stack(mean_v[0], prec_col)
    loads["points"].wait()
    for j in range(W):
        cols = slice(j * TW, (j + 1) * TW)
        d = jnp.exp2(tdot(sstack[0], target_stack(points_v[:, cols])))
        dens[:, cols] = d
        colpart[j] = jnp.sum(d, axis=0, keepdims=True)
    load(5, "values", values_h, values_v)
    load(6, "cash", cash_h, cash_v)
    load(7, "salvage", salvage_h, salvage_v)
    load(8, "cost", cost_h, cost_v)

    loads["cot"].wait()
    loads["dec"].wait()
    cot = cot_v[...]
    dec = dec_v[...]
    adj[0] = jnp.where(dec == 0, cot, 0.0) + pair_swap(jnp.where(dec == 1, cot, 0.0))

    pl.semaphore_wait(barrier, len(peers))
    far = Z > 2 * NEAR + 1
    if far:
        for i in (NEAR, -NEAR):
            pl.semaphore_signal(far_sem, inc=1, device_id=at_z(i), device_id_type=MESH)

    sends = []
    rs = []
    for i, k in plane:
        n = i * C + k
        rs.append(remote(colpart.at[place(i, k)], rs_buf.at[n], rs_send.at[n], rs_recv.at[n], at_w(i, k)))
    sends += rs

    gathers = {}
    for i in near_y:
        gathers[i] = [
            remote(mean_v.at[0], mean_v.at[i], g_send.at[i, 0], g_recv.at[i, 0], at_w(i, 0)),
            remote(adj.at[0], adj.at[i], g_send.at[i, 1], g_recv.at[i, 1], at_w(i, 0)),
        ]
        sends += gathers[i]

    width = min(128, Z * R)
    lane = lax.broadcasted_iota(jnp.int32, (F, width), 1)
    per = width // R
    for half in range(2):
        core = (c + 1 + half) % C
        blocks = []
        for g in range(Z // per):
            block = jnp.zeros((F, width), F32)
            for k in range(per):
                off = (g * per + k) * (W * R) + (y * C + core) * R
                base = pl.multiple_of(off // width * width, width)
                turn = (k * R + width - off % width) % width
                piece = pltpu.roll(points_v[:, pl.ds(base, width)], turn, 1)
                block = jnp.where((lane >= k * R) & (lane < (k + 1) * R), piece, block)
            blocks.append(block)
        t2[half] = target_stack(jnp.concatenate(blocks, axis=1))

    def back_block(i, half, first):
        d = jnp.exp2(tdot(t2[half], sstack[i]))
        hi, lo = split2(d)
        a = beside(adj[i])
        term = dot(hi, a) + dot(lo, a)
        acc[half] = term if first else acc[half] + term

    back_block(0, 0, True)
    back_block(0, 1, True)

    loads["values"].wait()
    for j in range(W):
        rows = slice(j * TW, (j + 1) * TW)
        vstack[rows, :] = beside(values_v[rows, :])

    for cp in rs:
        cp.wait_recv()
    total = colpart[w]
    for i, k in plane:
        total = total + rs_buf[i * C + k]
    zc_src[...] = total
    zc_buf[0] = total
    if far:
        pl.semaphore_wait(far_sem, 2)
    zc = []
    for i in far_first(Z):
        zc.append(remote(zc_src, zc_buf.at[i], zc_send.at[i], zc_recv.at[i], at_z(i)))
    sends += zc

    for n, i in enumerate(near_y):
        for cp in gathers[i]:
            cp.wait_recv()
        sstack[i] = source_stack(mean_v[i], prec_col)
        back_block(i, 0, False)
        if n == len(near_y) - 1:
            sib_src[...] = acc[0, :, :M] + acc[0, :, M:]
            sib = remote(sib_src, sib_buf, sib_send, sib_recv, at_w(0, 1))
            sends.append(sib)
        back_block(i, 1, False)
    own_v[...] = acc[1, :, :M] + acc[1, :, M:]
    sib.wait_recv()

    for o in range(Z):
        for side in range(2):
            half = (z + side) % 2
            rows = pl.ds(pl.multiple_of(((z + o) % Z) * R + half * (R // 2), R // 2), R // 2)
            z_src[side, o] = own_v[rows, :] + sib_buf[rows, :]
    z1 = [
        remote(z_src.at[0, pl.ds(1, H)], z1_buf.at[1], z1_send.at[0], z1_recv.at[1], at_z(1)),
        remote(z_src.at[1, pl.ds(Z - H, H)], z1_buf.at[0], z1_send.at[1], z1_recv.at[0], at_z(-1)),
    ]
    sends += z1

    for cp in zc:
        cp.wait_recv()
    total = zc_buf[0]
    for i in range(1, Z):
        total = total + zc_buf[i]
    col_all[w] = total
    ag = {}
    for i, k in plane:
        n = i * C + k
        ag[i, k] = remote(col_all.at[w], col_all.at[w], ag_send.at[n], ag_recv.at[n], at_w(i, k))
        sends.append(ag[i, k])

    def forward(chip, core):
        j = place(chip, core)
        cols = pl.ds(pl.multiple_of(j * TW, TW), TW)
        hi, lo = split2(dens[:, cols] * (scale / col_all[j]))
        v = vstack[cols, :]
        return dot(hi, v) + dot(lo, v)

    both = forward(0, 0)

    for cp in z1:
        cp.wait_recv()
    z2_src[0, 0] = z_src[0, 0] + z1_buf[0, H - 1]
    z2_src[1, 0] = z_src[1, 0] + z1_buf[1, 0]
    z2 = []
    for k in range(H - 1, 0, -1):
        z2_src[0, k] = z_src[0, Z - k] + z1_buf[0, H - 1 - k]
        z2_src[1, k] = z_src[1, k] + z1_buf[1, k]
        for side, dev in ((0, at_z(-k)), (1, at_z(k))):
            z2.append(
                remote(z2_src.at[side, k], z2_buf.at[side, k], z2_send.at[side, k], z2_recv.at[side, k], dev)
            )
    sends += z2

    for i, k in reversed(plane):
        ag[(Y - i) % Y, (C - k) % C].wait_recv()
        both = both + forward(i, k)

    xr_src[...] = (both[:, :M] + both[:, M:]).reshape(X, S4, M)
    xr = []
    for i in far_first(X):
        xr.append(remote(xr_src.at[(x + i) % X], xr_buf.at[i], xr_send.at[i], xr_recv.at[i], at_x(i)))
    sends += xr

    own_off = s * R
    win = min(128, TW)
    inner = own_off % TW
    base = pl.multiple_of(inner // win * win, win)
    line = col_all[own_off // TW, :, pl.ds(base, win)]
    r_iota = lax.broadcasted_iota(jnp.int32, (R, win), 0)
    l_iota = lax.broadcasted_iota(jnp.int32, (R, win), 1)
    own_sum = jnp.sum(jnp.where(l_iota == r_iota + inner % win, line, 0.0), axis=1, keepdims=True)
    own_factor = scale / own_sum

    loads["cash"].wait()
    loads["salvage"].wait()
    loads["cost"].wait()
    for cp in xr:
        cp.wait_recv()
    rows = pl.ds(pl.multiple_of(x * S4, S4), S4)
    hold = xr_src[x]
    for i in range(1, X):
        hold = hold + xr_buf[i]
    hold = hold + cash_v[rows, :]
    value_v[x] = jnp.maximum(jnp.maximum(hold, pair_swap(hold) - cost_v[...]), salvage_v[rows, :])
    xa = []
    for i in far_first(X):
        xa.append(remote(value_v.at[x], value_v.at[x], xa_send.at[i], xa_recv.at[i], at_x(i)))
    sends += xa

    for cp in z2:
        cp.wait_recv()
    parts = [z2_src[0, 0], z2_src[1, 0]]
    for k in range(1, H):
        parts[k % 2] = parts[k % 2] + z2_buf[0, k]
        parts[1 - k % 2] = parts[1 - k % 2] + z2_buf[1, k]
    for side in range(2):
        own_v[pl.ds(pl.multiple_of((z + side) % 2 * (R // 2), R // 2), R // 2), :] = parts[side]
    adjoint_out[0] = own_v[pl.ds(0, R), :] * own_factor

    for cp in xa:
        cp.wait_recv()
    value_out[...] = value_v[...].reshape(S, M)
    for cp in sends:
        cp.wait_send()


def on_device(dims, mean, points, precision, values, cash, salvage, cost, cot, dec):
    Z, Y, C, X = dims
    W = Y * C
    F, S = mean.shape
    T = points.shape[1]
    M = cot.shape[1]
    R, TW, K = T // (Z * W), T // W, 7 * F
    scale = float(S * Z * W) / float(T * X)
    hbm = pl.BlockSpec(memory_space=pltpu.HBM)
    vmem = pl.BlockSpec(memory_space=pltpu.VMEM)
    dma = pltpu.SemaphoreType.DMA
    H = Z // 2
    scratch = [
        pltpu.VMEM((Y, F, S), F32), pltpu.VMEM((Y, S, M), F32), pltpu.VMEM((S, M), F32), pltpu.VMEM((S, M), jnp.int32),
        pltpu.VMEM((F, T), F32), pltpu.VMEM((T, M), F32), pltpu.VMEM((S, M), F32), pltpu.VMEM((S, M), F32),
        pltpu.SMEM((F,), F32), pltpu.VMEM((1, M), F32),
        pltpu.VMEM((S, T), F32), pltpu.VMEM((Y, K, S), BF16), pltpu.VMEM((2, K, Z * R), BF16),
        pltpu.VMEM((T, 2 * M), BF16), pltpu.VMEM((2, Z * R, 2 * M), F32),
        pltpu.VMEM((W, 1, TW), F32), pltpu.VMEM((W, 1, TW), F32), pltpu.VMEM((1, TW), F32), pltpu.VMEM((Z, 1, TW), F32),
        pltpu.VMEM((W, 1, TW), F32),
        pltpu.VMEM((Z * R, M), F32), pltpu.VMEM((Z * R, M), F32), pltpu.VMEM((Z * R, M), F32),
        pltpu.VMEM((2, Z, R // 2, M), F32), pltpu.VMEM((2, H, R // 2, M), F32),
        pltpu.VMEM((2, H, R // 2, M), F32), pltpu.VMEM((2, H, R // 2, M), F32),
        pltpu.VMEM((X, S // X, M), F32), pltpu.VMEM((X, S // X, M), F32), pltpu.VMEM((X, S // X, M), F32),
        dma((9,)), dma((Y, 2)), dma((Y, 2)), dma((W,)), dma((W,)), dma((Z,)), dma((Z,)), dma((W,)), dma((W,)),
        dma, dma, dma((2,)), dma((2,)), dma((2, H)), dma((2, H)), dma((X,)), dma((X,)), dma((X,)), dma((X,)),
        pltpu.SemaphoreType.REGULAR,
    ]
    return pl.pallas_call(
        functools.partial(kernel, dims, scale),
        out_shape=(jax.ShapeDtypeStruct((S, M), F32), jax.ShapeDtypeStruct((1, R, M), F32)),
        in_specs=[hbm] * 9,
        out_specs=(vmem, vmem),
        scratch_shapes=scratch,
        compiler_params=pltpu.CompilerParams(
            collective_id=0, has_side_effects=True, vmem_limit_bytes=60 * 1024 * 1024
        ),
        name="mesh_step",
    )(mean, points, precision, values, cash, salvage, cost.reshape(1, M), cot, dec)


def build(mesh, dims):
    placed = (
        P(None, "src"), P(None, "tgt"), P(), P("tgt", None), P("src", None), P("src", None), P(), P("src", None),
        P("src", None),
    )
    return jax.shard_map(
        functools.partial(on_device, dims),
        mesh=mesh,
        in_specs=placed,
        out_specs=(P("src", None), P("tgt", "src", None)),
        check_vma=False,
    )


def solution(mesh):
    src, tgt = mesh.shape["src"], mesh.shape["tgt"]
    return build(mesh, (src // 8, 4, 2, tgt))
```

```python
import functools
import math

import jax
import jax.numpy as jnp
from jax import lax
from jax.experimental import pallas as pl
from jax.experimental.pallas import tpu as pltpu
from jax.sharding import PartitionSpec as P

F32, BF16 = jnp.float32, jnp.bfloat16
MESH = pl.DeviceIdType.MESH
LOG2E = math.log2(math.e)


def split2(v):
    hi = v.astype(BF16)
    return hi, (v - hi.astype(F32)).astype(BF16)


def split3(v):
    hi = v.astype(BF16)
    rest = v - hi.astype(F32)
    mid = rest.astype(BF16)
    return hi, mid, (rest - mid.astype(F32)).astype(BF16)


def beside(v):
    hi, lo = split2(v)
    return jnp.concatenate([hi, lo], axis=1)


def source_stack(mean, prec_col):
    scaled = mean * prec_col
    offset = jnp.sum(scaled * mean, axis=0, keepdims=True) * (-0.5 * LOG2E)
    a, b, c = split3(scaled * LOG2E)
    p, q, r = split3(offset)
    row = lax.broadcasted_iota(jnp.int32, mean.shape, 0)
    tail = jnp.where(
        row == 0, p.astype(F32), jnp.where(row == 1, q.astype(F32), jnp.where(row == 2, r.astype(F32), 0.0))
    ).astype(BF16)
    return jnp.concatenate([a, a, b, a, b, c, tail], axis=0)


def target_stack(points):
    a, b, c = split3(points)
    row = lax.broadcasted_iota(jnp.int32, points.shape, 0)
    tail = jnp.where(row < 3, 1.0, 0.0).astype(BF16)
    return jnp.concatenate([a, b, a, c, b, a, tail], axis=0)


def pair_swap(v):
    lane = lax.broadcasted_iota(jnp.int32, v.shape, 1)
    width = v.shape[1]
    return jnp.where(lane % 2 == 0, pltpu.roll(v, width - 1, 1), pltpu.roll(v, 1, 1))


def tdot(a, b):
    return lax.dot_general(a, b, (((0,), (0,)), ((), ())), preferred_element_type=F32)


def dot(a, b):
    return jnp.dot(a, b, preferred_element_type=F32)


def kernel(
    dims,
    scale,
    mean_h, points_h, prec_h, values_h, cash_h, salvage_h, cost_h, cot_h, dec_h,
    value_out, adjoint_out,
    mean_v, adj, cot_v, dec_v, points_v, values_v, cash_v, salvage_v, prec_s, cost_v,
    dens, sstack, t2, vstack, acc,
    colpart, rs_buf, zc_src, zc_buf, col_all,
    sib_src, sib_buf, own_v, z_src, z1_buf, z2_src, z2_buf,
    xr_src, xr_buf, value_v,
    ld_sem, g_send, g_recv, rs_send, rs_recv, zc_send, zc_recv, ag_send, ag_recv,
    sib_send, sib_recv, z1_send, z1_recv, z2_send, z2_recv, xr_send, xr_recv, xa_send, xa_recv, far_sem,
):
    Z, Y, C, X = dims
    W = Y * C
    S, M = cot_v.shape
    F, T = points_v.shape
    TW = T // W
    R = T // (Z * W)
    S4 = S // X
    H = Z // 2
    NEAR = 4
    s = lax.axis_index("src")
    x = lax.axis_index("tgt")
    z, w = s // W, s % W
    y, c = w // C, w % C

    def at_z(i):
        return (((z + i + Z) % Z) * W + w, x)

    def place(i, k):
        return ((y + i) % Y) * C + (c + k) % C

    def at_w(i, k):
        return (z * W + place(i, k), x)

    def at_x(i):
        return (s, (x + i) % X)

    def remote(src, dst, send, recv, dev):
        cp = pltpu.make_async_remote_copy(
            src_ref=src, dst_ref=dst, send_sem=send, recv_sem=recv, device_id=dev, device_id_type=MESH
        )
        cp.start()
        return cp

    def far_first(n):
        return sorted(range(1, n), key=lambda i: -min(i, n - i))

    near_y = sorted(range(1, Y), key=lambda i: min(i, Y - i))
    plane = [(i, k) for i in reversed(near_y) for k in range(C)] + [(0, k) for k in range(1, C)]

    loads = {}

    def load(k, name, src, dst):
        loads[name] = pltpu.make_async_copy(src, dst, ld_sem.at[k])
        loads[name].start()

    barrier = pltpu.get_barrier_semaphore()
    near_z = [i for i in far_first(Z) if min(i, Z - i) <= NEAR]
    peers = [at_z(i) for i in near_z] + [at_w(i, k) for i, k in plane] + [at_x(i) for i in far_first(X)]
    for dev in peers:
        pl.semaphore_signal(barrier, inc=1, device_id=dev, device_id_type=MESH)

    load(0, "prec", prec_h, prec_s)
    load(1, "mean", mean_h, mean_v.at[0])
    load(2, "points", points_h, points_v)
    load(3, "cot", cot_h, cot_v)
    load(4, "dec", dec_h, dec_v)

    loads["prec"].wait()
    loads["mean"].wait()
    frow = lax.broadcasted_iota(jnp.int32, (F, 1), 0)
    prec_col = jnp.zeros((F, 1), F32)
    for f in range(F):
        prec_col = jnp.where(frow == f, prec_s[f], prec_col)
    sstack[0] = source_stack(mean_v[0], prec_col)
    loads["points"].wait()
    for j in range(W):
        cols = slice(j * TW, (j + 1) * TW)
        d = jnp.exp2(tdot(sstack[0], target_stack(points_v[:, cols])))
        dens[:, cols] = d
        colpart[j] = jnp.sum(d, axis=0, keepdims=True)
    load(5, "values", values_h, values_v)
    load(6, "cash", cash_h, cash_v)
    load(7, "salvage", salvage_h, salvage_v)
    load(8, "cost", cost_h, cost_v)

    loads["cot"].wait()
    loads["dec"].wait()
    cot = cot_v[...]
    dec = dec_v[...]
    adj[0] = jnp.where(dec == 0, cot, 0.0) + pair_swap(jnp.where(dec == 1, cot, 0.0))

    pl.semaphore_wait(barrier, len(peers))
    far = Z > 2 * NEAR + 1
    if far:
        for i in (NEAR, -NEAR):
            pl.semaphore_signal(far_sem, inc=1, device_id=at_z(i), device_id_type=MESH)

    sends = []
    rs = []
    for i, k in plane:
        n = i * C + k
        rs.append(remote(colpart.at[place(i, k)], rs_buf.at[n], rs_send.at[n], rs_recv.at[n], at_w(i, k)))
    sends += rs

    gathers = {}
    for i in near_y:
        gathers[i] = [
            remote(mean_v.at[0], mean_v.at[i], g_send.at[i, 0], g_recv.at[i, 0], at_w(i, 0)),
            remote(adj.at[0], adj.at[i], g_send.at[i, 1], g_recv.at[i, 1], at_w(i, 0)),
        ]
        sends += gathers[i]

    width = min(128, Z * R)
    lane = lax.broadcasted_iota(jnp.int32, (F, width), 1)
    per = width // R
    for half in range(2):
        core = (c + 1 + half) % C
        blocks = []
        for g in range(Z // per):
            block = jnp.zeros((F, width), F32)
            for k in range(per):
                off = (g * per + k) * (W * R) + (y * C + core) * R
                base = pl.multiple_of(off // width * width, width)
                turn = (k * R + width - off % width) % width
                piece = pltpu.roll(points_v[:, pl.ds(base, width)], turn, 1)
                block = jnp.where((lane >= k * R) & (lane < (k + 1) * R), piece, block)
            blocks.append(block)
        t2[half] = target_stack(jnp.concatenate(blocks, axis=1))

    def back_block(i, half, first):
        d = jnp.exp2(tdot(t2[half], sstack[i]))
        hi, lo = split2(d)
        a = beside(adj[i])
        term = dot(hi, a) + dot(lo, a)
        acc[half] = term if first else acc[half] + term

    back_block(0, 0, True)
    back_block(0, 1, True)

    loads["values"].wait()
    for j in range(W):
        rows = slice(j * TW, (j + 1) * TW)
        vstack[rows, :] = beside(values_v[rows, :])

    for cp in rs:
        cp.wait_recv()
    total = colpart[w]
    for i, k in plane:
        total = total + rs_buf[i * C + k]
    zc_src[...] = total
    zc_buf[0] = total
    if far:
        pl.semaphore_wait(far_sem, 2)
    zc = []
    for i in far_first(Z):
        zc.append(remote(zc_src, zc_buf.at[i], zc_send.at[i], zc_recv.at[i], at_z(i)))
    sends += zc

    for n, i in enumerate(near_y):
        for cp in gathers[i]:
            cp.wait_recv()
        sstack[i] = source_stack(mean_v[i], prec_col)
        back_block(i, 0, False)
        if n == len(near_y) - 1:
            sib_src[...] = acc[0, :, :M] + acc[0, :, M:]
            sib = remote(sib_src, sib_buf, sib_send, sib_recv, at_w(0, 1))
            sends.append(sib)
        back_block(i, 1, False)
    own_v[...] = acc[1, :, :M] + acc[1, :, M:]
    for cp in zc:
        cp.wait_recv()
    total = zc_buf[0]
    for i in range(1, Z):
        total = total + zc_buf[i]
    col_all[w] = total
    ag = {}
    for i, k in plane:
        n = i * C + k
        ag[i, k] = remote(col_all.at[w], col_all.at[w], ag_send.at[n], ag_recv.at[n], at_w(i, k))
        sends.append(ag[i, k])

    sib.wait_recv()

    for o in range(Z):
        for side in range(2):
            half = (z + side) % 2
            rows = pl.ds(pl.multiple_of(((z + o) % Z) * R + half * (R // 2), R // 2), R // 2)
            z_src[side, o] = own_v[rows, :] + sib_buf[rows, :]
    z1 = [
        remote(z_src.at[0, pl.ds(1, H)], z1_buf.at[1], z1_send.at[0], z1_recv.at[1], at_z(1)),
        remote(z_src.at[1, pl.ds(Z - H, H)], z1_buf.at[0], z1_send.at[1], z1_recv.at[0], at_z(-1)),
    ]
    sends += z1

    def forward(chip, core):
        j = place(chip, core)
        cols = pl.ds(pl.multiple_of(j * TW, TW), TW)
        hi, lo = split2(dens[:, cols] * (scale / col_all[j]))
        v = vstack[cols, :]
        return dot(hi, v) + dot(lo, v)

    both = forward(0, 0)

    def forward_from(i, k):
        ag[(Y - i) % Y, (C - k) % C].wait_recv()
        return forward(i, k)

    for i, k in reversed(plane[C:]):
        both = both + forward_from(i, k)

    for cp in z1:
        cp.wait_recv()
    z2_src[0, 0] = z_src[0, 0] + z1_buf[0, H - 1]
    z2_src[1, 0] = z_src[1, 0] + z1_buf[1, 0]
    z2 = []
    for k in range(H - 1, 0, -1):
        z2_src[0, k] = z_src[0, Z - k] + z1_buf[0, H - 1 - k]
        z2_src[1, k] = z_src[1, k] + z1_buf[1, k]
        for side, dev in ((0, at_z(-k)), (1, at_z(k))):
            z2.append(
                remote(z2_src.at[side, k], z2_buf.at[side, k], z2_send.at[side, k], z2_recv.at[side, k], dev)
            )
    sends += z2

    for i, k in plane[:C]:
        both = both + forward_from(i, k)

    xr_src[...] = (both[:, :M] + both[:, M:]).reshape(X, S4, M)
    xr = []
    for i in far_first(X):
        xr.append(remote(xr_src.at[(x + i) % X], xr_buf.at[i], xr_send.at[i], xr_recv.at[i], at_x(i)))
    sends += xr

    own_off = s * R
    win = min(128, TW)
    inner = own_off % TW
    base = pl.multiple_of(inner // win * win, win)
    line = col_all[own_off // TW, :, pl.ds(base, win)]
    r_iota = lax.broadcasted_iota(jnp.int32, (R, win), 0)
    l_iota = lax.broadcasted_iota(jnp.int32, (R, win), 1)
    own_sum = jnp.sum(jnp.where(l_iota == r_iota + inner % win, line, 0.0), axis=1, keepdims=True)
    own_factor = scale / own_sum

    loads["cash"].wait()
    loads["salvage"].wait()
    loads["cost"].wait()
    for cp in xr:
        cp.wait_recv()
    rows = pl.ds(pl.multiple_of(x * S4, S4), S4)
    hold = xr_src[x]
    for i in range(1, X):
        hold = hold + xr_buf[i]
    hold = hold + cash_v[rows, :]
    value_v[x] = jnp.maximum(jnp.maximum(hold, pair_swap(hold) - cost_v[...]), salvage_v[rows, :])
    xa = []
    for i in far_first(X):
        xa.append(remote(value_v.at[x], value_v.at[x], xa_send.at[i], xa_recv.at[i], at_x(i)))
    sends += xa

    for cp in z2:
        cp.wait_recv()
    parts = [z2_src[0, 0], z2_src[1, 0]]
    for k in range(1, H):
        parts[k % 2] = parts[k % 2] + z2_buf[0, k]
        parts[1 - k % 2] = parts[1 - k % 2] + z2_buf[1, k]
    for side in range(2):
        own_v[pl.ds(pl.multiple_of((z + side) % 2 * (R // 2), R // 2), R // 2), :] = parts[side]
    adjoint_out[0] = own_v[pl.ds(0, R), :] * own_factor

    for cp in xa:
        cp.wait_recv()
    value_out[...] = value_v[...].reshape(S, M)
    for cp in sends:
        cp.wait_send()


def place_results(value_in, adjoint_in, value_out, adjoint_out, sem):
    copies = [
        pltpu.make_async_copy(value_in, value_out, sem.at[0]),
        pltpu.make_async_copy(adjoint_in, adjoint_out, sem.at[1]),
    ]
    for cp in copies:
        cp.start()
    for cp in copies:
        cp.wait()


def on_device(dims, mean, points, precision, values, cash, salvage, cost, cot, dec):
    Z, Y, C, X = dims
    W = Y * C
    F, S = mean.shape
    T = points.shape[1]
    M = cot.shape[1]
    R, TW, K = T // (Z * W), T // W, 7 * F
    scale = float(S * Z * W) / float(T * X)
    hbm = pl.BlockSpec(memory_space=pltpu.HBM)
    vmem = pl.BlockSpec(memory_space=pltpu.VMEM)
    dma = pltpu.SemaphoreType.DMA
    H = Z // 2
    scratch = [
        pltpu.VMEM((Y, F, S), F32), pltpu.VMEM((Y, S, M), F32), pltpu.VMEM((S, M), F32), pltpu.VMEM((S, M), jnp.int32),
        pltpu.VMEM((F, T), F32), pltpu.VMEM((T, M), F32), pltpu.VMEM((S, M), F32), pltpu.VMEM((S, M), F32),
        pltpu.SMEM((F,), F32), pltpu.VMEM((1, M), F32),
        pltpu.VMEM((S, T), F32), pltpu.VMEM((Y, K, S), BF16), pltpu.VMEM((2, K, Z * R), BF16),
        pltpu.VMEM((T, 2 * M), BF16), pltpu.VMEM((2, Z * R, 2 * M), F32),
        pltpu.VMEM((W, 1, TW), F32), pltpu.VMEM((W, 1, TW), F32), pltpu.VMEM((1, TW), F32), pltpu.VMEM((Z, 1, TW), F32),
        pltpu.VMEM((W, 1, TW), F32),
        pltpu.VMEM((Z * R, M), F32), pltpu.VMEM((Z * R, M), F32), pltpu.VMEM((Z * R, M), F32),
        pltpu.VMEM((2, Z, R // 2, M), F32), pltpu.VMEM((2, H, R // 2, M), F32),
        pltpu.VMEM((2, H, R // 2, M), F32), pltpu.VMEM((2, H, R // 2, M), F32),
        pltpu.VMEM((X, S // X, M), F32), pltpu.VMEM((X, S // X, M), F32), pltpu.VMEM((X, S // X, M), F32),
        dma((9,)), dma((Y, 2)), dma((Y, 2)), dma((W,)), dma((W,)), dma((Z,)), dma((Z,)), dma((W,)), dma((W,)),
        dma, dma, dma((2,)), dma((2,)), dma((2, H)), dma((2, H)), dma((X,)), dma((X,)), dma((X,)), dma((X,)),
        pltpu.SemaphoreType.REGULAR,
    ]
    shapes = (jax.ShapeDtypeStruct((S, M), F32), jax.ShapeDtypeStruct((1, R, M), F32))
    held = (pltpu.VMEM((S, M), F32), pltpu.VMEM((1, R, M), F32))
    results = pl.pallas_call(
        functools.partial(kernel, dims, scale),
        out_shape=held,
        in_specs=[hbm] * 9,
        out_specs=(vmem, vmem),
        scratch_shapes=scratch,
        compiler_params=pltpu.CompilerParams(
            collective_id=0, has_side_effects=True, vmem_limit_bytes=60 * 1024 * 1024
        ),
        name="mesh_step",
    )(mean, points, precision, values, cash, salvage, cost.reshape(1, M), cot, dec)
    return results


def build(mesh, dims):
    placed = (
        P(None, "src"), P(None, "tgt"), P(), P("tgt", None), P("src", None), P("src", None), P(), P("src", None),
        P("src", None),
    )
    return jax.shard_map(
        functools.partial(on_device, dims),
        mesh=mesh,
        in_specs=placed,
        out_specs=(P("src", None), P("tgt", "src", None)),
        check_vma=False,
    )


def solution(mesh):
    src, tgt = mesh.shape["src"], mesh.shape["tgt"]
    return build(mesh, (src // 8, 4, 2, tgt))
```

```python
import functools
import math

import jax
import jax.numpy as jnp
from jax import lax
from jax.experimental import pallas as pl
from jax.experimental.pallas import tpu as pltpu
from jax.sharding import PartitionSpec as P

F32, BF16 = jnp.float32, jnp.bfloat16
MESH = pl.DeviceIdType.MESH
LOG2E = math.log2(math.e)


def split2(v):
    hi = v.astype(BF16)
    return hi, (v - hi.astype(F32)).astype(BF16)


def split3(v):
    hi = v.astype(BF16)
    rest = v - hi.astype(F32)
    mid = rest.astype(BF16)
    return hi, mid, (rest - mid.astype(F32)).astype(BF16)


def beside(v):
    hi, lo = split2(v)
    return jnp.concatenate([hi, lo], axis=1)


def source_stack(mean, prec_col):
    scaled = mean * prec_col
    offset = jnp.sum(scaled * mean, axis=0, keepdims=True) * (-0.5 * LOG2E)
    a, b, c = split3(scaled * LOG2E)
    p, q, r = split3(offset)
    row = lax.broadcasted_iota(jnp.int32, mean.shape, 0)
    tail = jnp.where(
        row == 0, p.astype(F32), jnp.where(row == 1, q.astype(F32), jnp.where(row == 2, r.astype(F32), 0.0))
    ).astype(BF16)
    return jnp.concatenate([a, a, b, a, b, c, tail], axis=0)


def target_stack(points):
    a, b, c = split3(points)
    row = lax.broadcasted_iota(jnp.int32, points.shape, 0)
    tail = jnp.where(row < 3, 1.0, 0.0).astype(BF16)
    return jnp.concatenate([a, b, a, c, b, a, tail], axis=0)


def pair_swap(v):
    lane = lax.broadcasted_iota(jnp.int32, v.shape, 1)
    width = v.shape[1]
    return jnp.where(lane % 2 == 0, pltpu.roll(v, width - 1, 1), pltpu.roll(v, 1, 1))


def tdot(a, b):
    return lax.dot_general(a, b, (((0,), (0,)), ((), ())), preferred_element_type=F32)


def dot(a, b):
    return jnp.dot(a, b, preferred_element_type=F32)


def kernel(
    dims,
    scale,
    mean_h, points_h, prec_h, values_h, cash_h, salvage_h, cost_h, cot_h, dec_h,
    value_out, adjoint_out,
    mean_v, adj, cot_v, dec_v, points_v, values_v, cash_v, salvage_v, prec_s, cost_v,
    dens, sstack, t2, vstack, acc,
    colpart, rs_buf, zc_src, zc_buf, col_all,
    sib_src, sib_buf, own_v, z_src, z1_buf, z2_src, z2_buf,
    xr_src, xr_buf, value_v,
    ld_sem, g_send, g_recv, rs_send, rs_recv, zc_send, zc_recv, ag_send, ag_recv,
    sib_send, sib_recv, z1_send, z1_recv, z2_send, z2_recv, xr_send, xr_recv, xa_send, xa_recv, plane_sem, far_sem,
):
    Z, Y, C, X = dims
    W = Y * C
    S, M = cot_v.shape
    F, T = points_v.shape
    TW = T // W
    R = T // (Z * W)
    S4 = S // X
    H = Z // 2
    s = lax.axis_index("src")
    x = lax.axis_index("tgt")
    z, w = s // W, s % W
    y, c = w // C, w % C

    def at_z(i):
        return (((z + i + Z) % Z) * W + w, x)

    def place(i, k):
        return ((y + i) % Y) * C + (c + k) % C

    def at_w(i, k):
        return (z * W + place(i, k), x)

    def at_x(i):
        return (s, (x + i) % X)

    def remote(src, dst, send, recv, dev):
        cp = pltpu.make_async_remote_copy(
            src_ref=src, dst_ref=dst, send_sem=send, recv_sem=recv, device_id=dev, device_id_type=MESH
        )
        cp.start()
        return cp

    def far_first(n):
        return sorted(range(1, n), key=lambda i: -min(i, n - i))

    near_y = sorted(range(1, Y), key=lambda i: min(i, Y - i))
    plane = [(i, k) for i in reversed(near_y) for k in range(C)] + [(0, k) for k in range(1, C)]

    loads = {}

    def load(k, name, src, dst):
        loads[name] = pltpu.make_async_copy(src, dst, ld_sem.at[k])
        loads[name].start()

    barrier = pltpu.get_barrier_semaphore()
    def told(zz, yy, cc, xx):
        pl.semaphore_signal(barrier, inc=1, device_id=((zz * Y + yy) * C + cc, xx), device_id_type=MESH)

    for i in reversed(near_y):
        told(z, (y + i) % Y, 1, x)
    for i in far_first(X):
        told(z, y, 1, (x + i) % X)
    told(z, y, 1 - c, x)

    load(0, "prec", prec_h, prec_s)
    load(1, "mean", mean_h, mean_v.at[0])
    load(2, "points", points_h, points_v)
    load(3, "cot", cot_h, cot_v)
    load(4, "dec", dec_h, dec_v)

    for i in far_first(Z):
        told((z + i) % Z, y, 0, x)

    loads["prec"].wait()
    loads["mean"].wait()
    frow = lax.broadcasted_iota(jnp.int32, (F, 1), 0)
    prec_col = jnp.zeros((F, 1), F32)
    for f in range(F):
        prec_col = jnp.where(frow == f, prec_s[f], prec_col)
    sstack[0] = source_stack(mean_v[0], prec_col)
    loads["points"].wait()
    for j in range(W):
        cols = slice(j * TW, (j + 1) * TW)
        d = jnp.exp2(tdot(sstack[0], target_stack(points_v[:, cols])))
        dens[:, cols] = d
        colpart[j] = jnp.sum(d, axis=0, keepdims=True)
    load(5, "values", values_h, values_v)
    load(6, "cash", cash_h, cash_v)
    load(7, "salvage", salvage_h, salvage_v)
    load(8, "cost", cost_h, cost_v)

    loads["cot"].wait()
    loads["dec"].wait()
    cot = cot_v[...]
    dec = dec_v[...]
    adj[0] = jnp.where(dec == 0, cot, 0.0) + pair_swap(jnp.where(dec == 1, cot, 0.0))

    @pl.when(c == 1)
    def _():
        pl.semaphore_wait(barrier, 2 * (Y - 1) + 2 * (X - 1) + 1)
        pl.semaphore_signal(plane_sem, inc=1, device_id=at_w(0, 1), device_id_type=MESH)

    @pl.when(c == 0)
    def _():
        pl.semaphore_wait(plane_sem, 1)

    sends = []
    rs = []
    for i, k in plane:
        n = i * C + k
        rs.append(remote(colpart.at[place(i, k)], rs_buf.at[n], rs_send.at[n], rs_recv.at[n], at_w(i, k)))
    sends += rs

    gathers = {}
    for i in near_y:
        gathers[i] = [
            remote(mean_v.at[0], mean_v.at[i], g_send.at[i, 0], g_recv.at[i, 0], at_w(i, 0)),
            remote(adj.at[0], adj.at[i], g_send.at[i, 1], g_recv.at[i, 1], at_w(i, 0)),
        ]
        sends += gathers[i]

    width = min(128, Z * R)
    lane = lax.broadcasted_iota(jnp.int32, (F, width), 1)
    per = width // R
    for half in range(2):
        core = (c + 1 + half) % C
        blocks = []
        for g in range(Z // per):
            block = jnp.zeros((F, width), F32)
            for k in range(per):
                off = (g * per + k) * (W * R) + (y * C + core) * R
                base = pl.multiple_of(off // width * width, width)
                turn = (k * R + width - off % width) % width
                piece = pltpu.roll(points_v[:, pl.ds(base, width)], turn, 1)
                block = jnp.where((lane >= k * R) & (lane < (k + 1) * R), piece, block)
            blocks.append(block)
        t2[half] = target_stack(jnp.concatenate(blocks, axis=1))

    def back_block(i, half, first):
        d = jnp.exp2(tdot(t2[half], sstack[i]))
        hi, lo = split2(d)
        a = beside(adj[i])
        term = dot(hi, a) + dot(lo, a)
        acc[half] = term if first else acc[half] + term

    back_block(0, 0, True)
    back_block(0, 1, True)

    loads["values"].wait()
    for j in range(W):
        rows = slice(j * TW, (j + 1) * TW)
        vstack[rows, :] = beside(values_v[rows, :])

    @pl.when(c == 0)
    def _():
        pl.semaphore_wait(barrier, 2 * (Z - 1) + 1)
        pl.semaphore_signal(far_sem, inc=1, device_id=at_w(0, 1), device_id_type=MESH)

    for cp in rs:
        cp.wait_recv()
    total = colpart[w]
    for i, k in plane:
        total = total + rs_buf[i * C + k]
    zc_src[...] = total
    zc_buf[0] = total
    @pl.when(c == 1)
    def _():
        pl.semaphore_wait(far_sem, 1)

    zc = []
    for i in far_first(Z):
        zc.append(remote(zc_src, zc_buf.at[i], zc_send.at[i], zc_recv.at[i], at_z(i)))
    sends += zc

    for n, i in enumerate(near_y):
        for cp in gathers[i]:
            cp.wait_recv()
        sstack[i] = source_stack(mean_v[i], prec_col)
        back_block(i, 0, False)
        if n == len(near_y) - 1:
            sib_src[...] = acc[0, :, :M] + acc[0, :, M:]
            sib = remote(sib_src, sib_buf, sib_send, sib_recv, at_w(0, 1))
            sends.append(sib)
        back_block(i, 1, False)
    own_v[...] = acc[1, :, :M] + acc[1, :, M:]
    for cp in zc:
        cp.wait_recv()
    total = zc_buf[0]
    for i in range(1, Z):
        total = total + zc_buf[i]
    col_all[w] = total
    ag = {}
    for i, k in plane:
        n = i * C + k
        ag[i, k] = remote(col_all.at[w], col_all.at[w], ag_send.at[n], ag_recv.at[n], at_w(i, k))
        sends.append(ag[i, k])

    sib.wait_recv()

    for o in range(Z):
        for side in range(2):
            half = (z + side) % 2
            rows = pl.ds(pl.multiple_of(((z + o) % Z) * R + half * (R // 2), R // 2), R // 2)
            z_src[side, o] = own_v[rows, :] + sib_buf[rows, :]
    z1 = [
        remote(z_src.at[0, pl.ds(1, H)], z1_buf.at[1], z1_send.at[0], z1_recv.at[1], at_z(1)),
        remote(z_src.at[1, pl.ds(Z - H, H)], z1_buf.at[0], z1_send.at[1], z1_recv.at[0], at_z(-1)),
    ]
    sends += z1

    def forward(chip, core):
        j = place(chip, core)
        cols = pl.ds(pl.multiple_of(j * TW, TW), TW)
        hi, lo = split2(dens[:, cols] * (scale / col_all[j]))
        v = vstack[cols, :]
        return dot(hi, v) + dot(lo, v)

    both = forward(0, 0)

    def forward_from(i, k):
        ag[(Y - i) % Y, (C - k) % C].wait_recv()
        return forward(i, k)

    for i, k in reversed(plane[C:]):
        both = both + forward_from(i, k)

    for i, k in plane[:C]:
        both = both + forward_from(i, k)

    xr_src[...] = (both[:, :M] + both[:, M:]).reshape(X, S4, M)
    xr = []
    for i in far_first(X):
        xr.append(remote(xr_src.at[(x + i) % X], xr_buf.at[i], xr_send.at[i], xr_recv.at[i], at_x(i)))
    for cp in sends:
        cp.wait_send()

    for cp in z1:
        cp.wait_recv()
    z2_src[0, 0] = z_src[0, 0] + z1_buf[0, H - 1]
    z2_src[1, 0] = z_src[1, 0] + z1_buf[1, 0]
    z2 = []
    for k in range(H - 1, 0, -1):
        z2_src[0, k] = z_src[0, Z - k] + z1_buf[0, H - 1 - k]
        z2_src[1, k] = z_src[1, k] + z1_buf[1, k]
        for side, dev in ((0, at_z(-k)), (1, at_z(k))):
            z2.append(
                remote(z2_src.at[side, k], z2_buf.at[side, k], z2_send.at[side, k], z2_recv.at[side, k], dev)
            )
    sends += z2

    own_off = s * R
    win = min(128, TW)
    inner = own_off % TW
    base = pl.multiple_of(inner // win * win, win)
    line = col_all[own_off // TW, :, pl.ds(base, win)]
    r_iota = lax.broadcasted_iota(jnp.int32, (R, win), 0)
    l_iota = lax.broadcasted_iota(jnp.int32, (R, win), 1)
    own_sum = jnp.sum(jnp.where(l_iota == r_iota + inner % win, line, 0.0), axis=1, keepdims=True)
    own_factor = scale / own_sum

    loads["cash"].wait()
    loads["salvage"].wait()
    loads["cost"].wait()
    for cp in xr:
        cp.wait_recv()
    rows = pl.ds(pl.multiple_of(x * S4, S4), S4)
    hold = xr_src[x]
    for i in range(1, X):
        hold = hold + xr_buf[i]
    hold = hold + cash_v[rows, :]
    value_v[x] = jnp.maximum(jnp.maximum(hold, pair_swap(hold) - cost_v[...]), salvage_v[rows, :])
    xa = []
    for i in far_first(X):
        xa.append(remote(value_v.at[x], value_v.at[x], xa_send.at[i], xa_recv.at[i], at_x(i)))
    for cp in xr + z2:
        cp.wait_send()

    for cp in z2:
        cp.wait_recv()
    parts = [z2_src[0, 0], z2_src[1, 0]]
    for k in range(1, H):
        parts[k % 2] = parts[k % 2] + z2_buf[0, k]
        parts[1 - k % 2] = parts[1 - k % 2] + z2_buf[1, k]
    for side in range(2):
        own_v[pl.ds(pl.multiple_of((z + side) % 2 * (R // 2), R // 2), R // 2), :] = parts[side]
    adjoint_out[0] = own_v[pl.ds(0, R), :] * own_factor

    for cp in xa:
        cp.wait_recv()
    value_out[...] = value_v[...].reshape(S, M)
    for cp in xa:
        cp.wait_send()


def place_results(value_in, adjoint_in, value_out, adjoint_out, sem):
    copies = [
        pltpu.make_async_copy(value_in, value_out, sem.at[0]),
        pltpu.make_async_copy(adjoint_in, adjoint_out, sem.at[1]),
    ]
    for cp in copies:
        cp.start()
    for cp in copies:
        cp.wait()


def on_device(dims, mean, points, precision, values, cash, salvage, cost, cot, dec):
    Z, Y, C, X = dims
    W = Y * C
    F, S = mean.shape
    T = points.shape[1]
    M = cot.shape[1]
    R, TW, K = T // (Z * W), T // W, 7 * F
    scale = float(S * Z * W) / float(T * X)
    hbm = pl.BlockSpec(memory_space=pltpu.HBM)
    vmem = pl.BlockSpec(memory_space=pltpu.VMEM)
    dma = pltpu.SemaphoreType.DMA
    H = Z // 2
    scratch = [
        pltpu.VMEM((Y, F, S), F32), pltpu.VMEM((Y, S, M), F32), pltpu.VMEM((S, M), F32), pltpu.VMEM((S, M), jnp.int32),
        pltpu.VMEM((F, T), F32), pltpu.VMEM((T, M), F32), pltpu.VMEM((S, M), F32), pltpu.VMEM((S, M), F32),
        pltpu.SMEM((F,), F32), pltpu.VMEM((1, M), F32),
        pltpu.VMEM((S, T), F32), pltpu.VMEM((Y, K, S), BF16), pltpu.VMEM((2, K, Z * R), BF16),
        pltpu.VMEM((T, 2 * M), BF16), pltpu.VMEM((2, Z * R, 2 * M), F32),
        pltpu.VMEM((W, 1, TW), F32), pltpu.VMEM((W, 1, TW), F32), pltpu.VMEM((1, TW), F32), pltpu.VMEM((Z, 1, TW), F32),
        pltpu.VMEM((W, 1, TW), F32),
        pltpu.VMEM((Z * R, M), F32), pltpu.VMEM((Z * R, M), F32), pltpu.VMEM((Z * R, M), F32),
        pltpu.VMEM((2, Z, R // 2, M), F32), pltpu.VMEM((2, H, R // 2, M), F32),
        pltpu.VMEM((2, H, R // 2, M), F32), pltpu.VMEM((2, H, R // 2, M), F32),
        pltpu.VMEM((X, S // X, M), F32), pltpu.VMEM((X, S // X, M), F32), pltpu.VMEM((X, S // X, M), F32),
        dma((9,)), dma((Y, 2)), dma((Y, 2)), dma((W,)), dma((W,)), dma((Z,)), dma((Z,)), dma((W,)), dma((W,)),
        dma, dma, dma((2,)), dma((2,)), dma((2, H)), dma((2, H)), dma((X,)), dma((X,)), dma((X,)), dma((X,)),
        pltpu.SemaphoreType.REGULAR, pltpu.SemaphoreType.REGULAR,
    ]
    shapes = (jax.ShapeDtypeStruct((S, M), F32), jax.ShapeDtypeStruct((1, R, M), F32))
    held = (pltpu.VMEM((S, M), F32), pltpu.VMEM((1, R, M), F32))
    results = pl.pallas_call(
        functools.partial(kernel, dims, scale),
        out_shape=held,
        in_specs=[hbm] * 9,
        out_specs=(vmem, vmem),
        scratch_shapes=scratch,
        compiler_params=pltpu.CompilerParams(
            collective_id=0, has_side_effects=True, vmem_limit_bytes=60 * 1024 * 1024
        ),
        name="mesh_step",
    )(mean, points, precision, values, cash, salvage, cost.reshape(1, M), cot, dec)
    return results


def build(mesh, dims):
    placed = (
        P(None, "src"), P(None, "tgt"), P(), P("tgt", None), P("src", None), P("src", None), P(), P("src", None),
        P("src", None),
    )
    return jax.shard_map(
        functools.partial(on_device, dims),
        mesh=mesh,
        in_specs=placed,
        out_specs=(P("src", None), P("tgt", "src", None)),
        check_vma=False,
    )


def solution(mesh):
    src, tgt = mesh.shape["src"], mesh.shape["tgt"]
    return build(mesh, (src // 8, 4, 2, tgt))
```

```python
import functools
import math

import jax
import jax.numpy as jnp
from jax import lax
from jax.experimental import pallas as pl
from jax.experimental.pallas import tpu as pltpu
from jax.sharding import PartitionSpec as P

F32, BF16 = jnp.float32, jnp.bfloat16
MESH = pl.DeviceIdType.MESH
LOG2E = math.log2(math.e)


def split2(v):
    hi = v.astype(BF16)
    return hi, (v - hi.astype(F32)).astype(BF16)


def split3(v):
    hi = v.astype(BF16)
    rest = v - hi.astype(F32)
    mid = rest.astype(BF16)
    return hi, mid, (rest - mid.astype(F32)).astype(BF16)


def beside(v):
    hi, lo = split2(v)
    return jnp.concatenate([hi, lo], axis=1)


def source_stack(mean, prec_col):
    scaled = mean * prec_col
    offset = jnp.sum(scaled * mean, axis=0, keepdims=True) * (-0.5 * LOG2E)
    a, b, c = split3(scaled * LOG2E)
    p, q, r = split3(offset)
    row = lax.broadcasted_iota(jnp.int32, mean.shape, 0)
    tail = jnp.where(
        row == 0, p.astype(F32), jnp.where(row == 1, q.astype(F32), jnp.where(row == 2, r.astype(F32), 0.0))
    ).astype(BF16)
    return jnp.concatenate([a, a, b, a, b, c, tail], axis=0)


def target_stack(points):
    a, b, c = split3(points)
    row = lax.broadcasted_iota(jnp.int32, points.shape, 0)
    tail = jnp.where(row < 3, 1.0, 0.0).astype(BF16)
    return jnp.concatenate([a, b, a, c, b, a, tail], axis=0)


def pair_swap(v):
    lane = lax.broadcasted_iota(jnp.int32, v.shape, 1)
    width = v.shape[1]
    return jnp.where(lane % 2 == 0, pltpu.roll(v, width - 1, 1), pltpu.roll(v, 1, 1))


def tdot(a, b):
    return lax.dot_general(a, b, (((0,), (0,)), ((), ())), preferred_element_type=F32)


def dot(a, b):
    return jnp.dot(a, b, preferred_element_type=F32)


def kernel(
    dims,
    scale,
    mean_h, points_h, prec_h, values_h, cash_h, salvage_h, cost_h, cot_h, dec_h,
    value_out, adjoint_out,
    mean_v, adj, cot_v, dec_v, points_v, values_v, cash_v, salvage_v, prec_s, cost_v,
    dens, sstack, t2, vstack, acc,
    colpart, rs_buf, zc_src, zc_buf, col_all,
    sib_src, sib_buf, own_v, z_src, z1_buf, z2_src, z2_buf,
    xr_src, xr_buf, value_v,
    ld_sem, g_send, g_recv, rs_send, rs_recv, zc_send, zc_recv, ag_send, ag_recv,
    sib_send, sib_recv, z1_send, z1_recv, z2_send, z2_recv, xr_send, xr_recv, xa_send, xa_recv, plane_sem, far_sem,
):
    Z, Y, C, X = dims
    W = Y * C
    S, M = cot_v.shape
    F, T = points_v.shape
    TW = T // W
    R = T // (Z * W)
    S4 = S // X
    H = Z // 2
    s = lax.axis_index("src")
    x = lax.axis_index("tgt")
    z, w = s // W, s % W
    y, c = w // C, w % C

    def at_z(i):
        return (((z + i + Z) % Z) * W + w, x)

    def place(i, k):
        return ((y + i) % Y) * C + (c + k) % C

    def at_w(i, k):
        return (z * W + place(i, k), x)

    def at_x(i):
        return (s, (x + i) % X)

    def remote(src, dst, send, recv, dev):
        cp = pltpu.make_async_remote_copy(
            src_ref=src, dst_ref=dst, send_sem=send, recv_sem=recv, device_id=dev, device_id_type=MESH
        )
        cp.start()
        return cp

    def far_first(n):
        return sorted(range(1, n), key=lambda i: -min(i, n - i))

    near_y = sorted(range(1, Y), key=lambda i: min(i, Y - i))
    plane = [(i, k) for i in reversed(near_y) for k in range(C)] + [(0, k) for k in range(1, C)]

    loads = {}

    def load(k, name, src, dst):
        loads[name] = pltpu.make_async_copy(src, dst, ld_sem.at[k])
        loads[name].start()

    barrier = pltpu.get_barrier_semaphore()
    def told(zz, yy, cc, xx):
        pl.semaphore_signal(barrier, inc=1, device_id=((zz * Y + yy) * C + cc, xx), device_id_type=MESH)

    for i in reversed(near_y):
        told(z, (y + i) % Y, 1, x)
    for i in far_first(X):
        told(z, y, 1, (x + i) % X)
    told(z, y, 1 - c, x)

    load(0, "prec", prec_h, prec_s)
    load(1, "mean", mean_h, mean_v.at[0])
    load(2, "points", points_h, points_v)
    load(3, "cot", cot_h, cot_v)
    load(4, "dec", dec_h, dec_v)

    for i in far_first(Z):
        told((z + i) % Z, y, 0, x)

    loads["prec"].wait()
    loads["mean"].wait()
    frow = lax.broadcasted_iota(jnp.int32, (F, 1), 0)
    prec_col = jnp.zeros((F, 1), F32)
    for f in range(F):
        prec_col = jnp.where(frow == f, prec_s[f], prec_col)
    sstack[0] = source_stack(mean_v[0], prec_col)
    loads["points"].wait()
    for j in range(W):
        cols = slice(j * TW, (j + 1) * TW)
        d = jnp.exp2(tdot(sstack[0], target_stack(points_v[:, cols])))
        dens[:, cols] = d
        colpart[j] = jnp.sum(d, axis=0, keepdims=True)
    load(5, "values", values_h, values_v)
    load(6, "cash", cash_h, cash_v)
    load(7, "salvage", salvage_h, salvage_v)
    load(8, "cost", cost_h, cost_v)

    loads["cot"].wait()
    loads["dec"].wait()
    cot = cot_v[...]
    dec = dec_v[...]
    adj[0] = jnp.where(dec == 0, cot, 0.0) + pair_swap(jnp.where(dec == 1, cot, 0.0))

    @pl.when(c == 1)
    def _():
        pl.semaphore_wait(barrier, 2 * (Y - 1) + 2 * (X - 1) + 1)
        pl.semaphore_signal(plane_sem, inc=1, device_id=at_w(0, 1), device_id_type=MESH)

    @pl.when(c == 0)
    def _():
        pl.semaphore_wait(plane_sem, 1)

    sends = []
    rs = []
    for i, k in plane:
        n = i * C + k
        rs.append(remote(colpart.at[place(i, k)], rs_buf.at[n], rs_send.at[n], rs_recv.at[n], at_w(i, k)))
    sends += rs

    gathers = {}
    for i in near_y:
        gathers[i] = [
            remote(mean_v.at[0], mean_v.at[i], g_send.at[i, 0], g_recv.at[i, 0], at_w(i, 0)),
            remote(adj.at[0], adj.at[i], g_send.at[i, 1], g_recv.at[i, 1], at_w(i, 0)),
        ]
        sends += gathers[i]

    width = min(128, Z * R)
    lane = lax.broadcasted_iota(jnp.int32, (F, width), 1)
    per = width // R
    for half in range(2):
        core = (c + 1 + half) % C
        blocks = []
        for g in range(Z // per):
            block = jnp.zeros((F, width), F32)
            for k in range(per):
                off = (g * per + k) * (W * R) + (y * C + core) * R
                base = pl.multiple_of(off // width * width, width)
                turn = (k * R + width - off % width) % width
                piece = pltpu.roll(points_v[:, pl.ds(base, width)], turn, 1)
                block = jnp.where((lane >= k * R) & (lane < (k + 1) * R), piece, block)
            blocks.append(block)
        t2[half] = target_stack(jnp.concatenate(blocks, axis=1))

    def back_block(i, half, first):
        d = jnp.exp2(tdot(t2[half], sstack[i]))
        hi, lo = split2(d)
        a = beside(adj[i])
        term = dot(hi, a) + dot(lo, a)
        acc[half] = term if first else acc[half] + term

    back_block(0, 0, True)
    back_block(0, 1, True)

    loads["values"].wait()
    for j in range(W):
        rows = slice(j * TW, (j + 1) * TW)
        vstack[rows, :] = beside(values_v[rows, :])

    @pl.when(c == 0)
    def _():
        pl.semaphore_wait(barrier, 2 * (Z - 1) + 1)
        pl.semaphore_signal(far_sem, inc=1, device_id=at_w(0, 1), device_id_type=MESH)

    for cp in rs:
        cp.wait_recv()
    total = colpart[w]
    for i, k in plane:
        total = total + rs_buf[i * C + k]
    zc_src[...] = total
    zc_buf[0] = total
    @pl.when(c == 1)
    def _():
        pl.semaphore_wait(far_sem, 1)

    zc = []
    for i in far_first(Z):
        zc.append(remote(zc_src, zc_buf.at[i], zc_send.at[i], zc_recv.at[i], at_z(i)))
    sends += zc

    for n, i in enumerate(near_y):
        for cp in gathers[i]:
            cp.wait_recv()
        sstack[i] = source_stack(mean_v[i], prec_col)
        back_block(i, 0, False)
        if n == len(near_y) - 1:
            sib_src[...] = acc[0, :, :M] + acc[0, :, M:]
            sib = remote(sib_src, sib_buf, sib_send, sib_recv, at_w(0, 1))
            sends.append(sib)
        back_block(i, 1, False)
    own_v[...] = acc[1, :, :M] + acc[1, :, M:]
    for cp in zc:
        cp.wait_recv()
    total = zc_buf[0]
    for i in range(1, Z):
        total = total + zc_buf[i]
    col_all[w] = total
    ag = {}
    for i, k in plane:
        n = i * C + k
        ag[i, k] = remote(col_all.at[w], col_all.at[w], ag_send.at[n], ag_recv.at[n], at_w(i, k))
        sends.append(ag[i, k])

    sib.wait_recv()

    for o in range(Z):
        for side in range(2):
            half = (z + side) % 2
            rows = pl.ds(pl.multiple_of(((z + o) % Z) * R + half * (R // 2), R // 2), R // 2)
            z_src[side, o] = own_v[rows, :] + sib_buf[rows, :]
    z1 = [
        remote(z_src.at[0, pl.ds(1, H)], z1_buf.at[1], z1_send.at[0], z1_recv.at[1], at_z(1)),
        remote(z_src.at[1, pl.ds(Z - H, H)], z1_buf.at[0], z1_send.at[1], z1_recv.at[0], at_z(-1)),
    ]
    sends += z1

    def forward(chip, core):
        j = place(chip, core)
        cols = pl.ds(pl.multiple_of(j * TW, TW), TW)
        hi, lo = split2(dens[:, cols] * (scale / col_all[j]))
        v = vstack[cols, :]
        return dot(hi, v) + dot(lo, v)

    both = forward(0, 0)

    def forward_from(i, k):
        ag[(Y - i) % Y, (C - k) % C].wait_recv()
        return forward(i, k)

    for i, k in reversed(plane[C:]):
        both = both + forward_from(i, k)

    for i, k in plane[:C]:
        both = both + forward_from(i, k)

    xr_src[...] = (both[:, :M] + both[:, M:]).reshape(X, S4, M)
    xr = []
    for i in far_first(X):
        xr.append(remote(xr_src.at[(x + i) % X], xr_buf.at[i], xr_send.at[i], xr_recv.at[i], at_x(i)))
    for cp in z1:
        cp.wait_recv()
    z2_src[0, 0] = z_src[0, 0] + z1_buf[0, H - 1]
    z2_src[1, 0] = z_src[1, 0] + z1_buf[1, 0]
    z2 = []
    for k in range(H - 1, 0, -1):
        z2_src[0, k] = z_src[0, Z - k] + z1_buf[0, H - 1 - k]
        z2_src[1, k] = z_src[1, k] + z1_buf[1, k]
        for side, dev in ((0, at_z(-k)), (1, at_z(k))):
            z2.append(
                remote(z2_src.at[side, k], z2_buf.at[side, k], z2_send.at[side, k], z2_recv.at[side, k], dev)
            )

    for cp in sends:
        cp.wait_send()

    own_off = s * R
    win = min(128, TW)
    inner = own_off % TW
    base = pl.multiple_of(inner // win * win, win)
    line = col_all[own_off // TW, :, pl.ds(base, win)]
    r_iota = lax.broadcasted_iota(jnp.int32, (R, win), 0)
    l_iota = lax.broadcasted_iota(jnp.int32, (R, win), 1)
    own_sum = jnp.sum(jnp.where(l_iota == r_iota + inner % win, line, 0.0), axis=1, keepdims=True)
    own_factor = scale / own_sum

    loads["cash"].wait()
    loads["salvage"].wait()
    loads["cost"].wait()
    for cp in xr:
        cp.wait_recv()
    rows = pl.ds(pl.multiple_of(x * S4, S4), S4)
    hold = xr_src[x]
    for i in range(1, X):
        hold = hold + xr_buf[i]
    hold = hold + cash_v[rows, :]
    value_v[x] = jnp.maximum(jnp.maximum(hold, pair_swap(hold) - cost_v[...]), salvage_v[rows, :])
    xa = []
    for i in far_first(X):
        xa.append(remote(value_v.at[x], value_v.at[x], xa_send.at[i], xa_recv.at[i], at_x(i)))
    for cp in xr + z2:
        cp.wait_send()

    for cp in z2:
        cp.wait_recv()
    parts = [z2_src[0, 0], z2_src[1, 0]]
    for k in range(1, H):
        parts[k % 2] = parts[k % 2] + z2_buf[0, k]
        parts[1 - k % 2] = parts[1 - k % 2] + z2_buf[1, k]
    for side in range(2):
        own_v[pl.ds(pl.multiple_of((z + side) % 2 * (R // 2), R // 2), R // 2), :] = parts[side]
    adjoint_out[0] = own_v[pl.ds(0, R), :] * own_factor

    for cp in xa:
        cp.wait_recv()
    value_out[...] = value_v[...].reshape(S, M)
    for cp in xa:
        cp.wait_send()


def place_results(value_in, adjoint_in, value_out, adjoint_out, sem):
    copies = [
        pltpu.make_async_copy(value_in, value_out, sem.at[0]),
        pltpu.make_async_copy(adjoint_in, adjoint_out, sem.at[1]),
    ]
    for cp in copies:
        cp.start()
    for cp in copies:
        cp.wait()


def on_device(dims, mean, points, precision, values, cash, salvage, cost, cot, dec):
    Z, Y, C, X = dims
    W = Y * C
    F, S = mean.shape
    T = points.shape[1]
    M = cot.shape[1]
    R, TW, K = T // (Z * W), T // W, 7 * F
    scale = float(S * Z * W) / float(T * X)
    hbm = pl.BlockSpec(memory_space=pltpu.HBM)
    vmem = pl.BlockSpec(memory_space=pltpu.VMEM)
    dma = pltpu.SemaphoreType.DMA
    H = Z // 2
    scratch = [
        pltpu.VMEM((Y, F, S), F32), pltpu.VMEM((Y, S, M), F32), pltpu.VMEM((S, M), F32), pltpu.VMEM((S, M), jnp.int32),
        pltpu.VMEM((F, T), F32), pltpu.VMEM((T, M), F32), pltpu.VMEM((S, M), F32), pltpu.VMEM((S, M), F32),
        pltpu.SMEM((F,), F32), pltpu.VMEM((1, M), F32),
        pltpu.VMEM((S, T), F32), pltpu.VMEM((Y, K, S), BF16), pltpu.VMEM((2, K, Z * R), BF16),
        pltpu.VMEM((T, 2 * M), BF16), pltpu.VMEM((2, Z * R, 2 * M), F32),
        pltpu.VMEM((W, 1, TW), F32), pltpu.VMEM((W, 1, TW), F32), pltpu.VMEM((1, TW), F32), pltpu.VMEM((Z, 1, TW), F32),
        pltpu.VMEM((W, 1, TW), F32),
        pltpu.VMEM((Z * R, M), F32), pltpu.VMEM((Z * R, M), F32), pltpu.VMEM((Z * R, M), F32),
        pltpu.VMEM((2, Z, R // 2, M), F32), pltpu.VMEM((2, H, R // 2, M), F32),
        pltpu.VMEM((2, H, R // 2, M), F32), pltpu.VMEM((2, H, R // 2, M), F32),
        pltpu.VMEM((X, S // X, M), F32), pltpu.VMEM((X, S // X, M), F32), pltpu.VMEM((X, S // X, M), F32),
        dma((9,)), dma((Y, 2)), dma((Y, 2)), dma((W,)), dma((W,)), dma((Z,)), dma((Z,)), dma((W,)), dma((W,)),
        dma, dma, dma((2,)), dma((2,)), dma((2, H)), dma((2, H)), dma((X,)), dma((X,)), dma((X,)), dma((X,)),
        pltpu.SemaphoreType.REGULAR, pltpu.SemaphoreType.REGULAR,
    ]
    shapes = (jax.ShapeDtypeStruct((S, M), F32), jax.ShapeDtypeStruct((1, R, M), F32))
    held = (pltpu.VMEM((S, M), F32), pltpu.VMEM((1, R, M), F32))
    results = pl.pallas_call(
        functools.partial(kernel, dims, scale),
        out_shape=held,
        in_specs=[hbm] * 9,
        out_specs=(vmem, vmem),
        scratch_shapes=scratch,
        compiler_params=pltpu.CompilerParams(
            collective_id=0, has_side_effects=True, vmem_limit_bytes=60 * 1024 * 1024
        ),
        name="mesh_step",
    )(mean, points, precision, values, cash, salvage, cost.reshape(1, M), cot, dec)
    return results


def build(mesh, dims):
    placed = (
        P(None, "src"), P(None, "tgt"), P(), P("tgt", None), P("src", None), P("src", None), P(), P("src", None),
        P("src", None),
    )
    return jax.shard_map(
        functools.partial(on_device, dims),
        mesh=mesh,
        in_specs=placed,
        out_specs=(P("src", None), P("tgt", "src", None)),
        check_vma=False,
    )


def solution(mesh):
    src, tgt = mesh.shape["src"], mesh.shape["tgt"]
    return build(mesh, (src // 8, 4, 2, tgt))
```
